32 devices in a mesh: tok: 4 (over y, x), feat: 8 (over z, core).
Axes of the slice: x: 2, y: 2, z: 4, core: 2. Of those that a mesh axis runs over, the one named last changes fastest.
Arguments:
- tokens: bfloat16 [256, 8192], P('tok', 'feat'), may hold values from -6 to 6
- gain: float32 [8192], replicated, may hold values from 0.1 to 1.9
- proj: bfloat16 [8192, 8192], P('tok', 'feat'), may hold values from -0.0625 to 0.0625
- panel_index: int32 [1], replicated, may hold values from 0 to 31
Outputs:
- panel_rows: float32 [256, 8192], P(None, 'feat')
- solved_cross: float32 [256, 8192], P(None, 'feat')
The draws below stay inside these ranges and needn't reach their ends.
All inputs are finite; a program needn't handle non-finite values.
Results may differ from the reference program's by a relative error of at most 0.01.
Values may be sent and summed in bfloat16 or wider, within the bound.
A program may use at most 64 MiB of HBM per device.

```python
import math
import jax
import jax.numpy as jnp
from jax import lax

D = 8192
PANEL = 256
TOKENS = 256


def steps_of(own_key, dims, shards, low, largest):
    level, own = 1.0, jax.random.fold_in(own_key, 6)
    for axis_at, blocks in shards:
        draws = jnp.exp(jax.random.uniform(jax.random.fold_in(own, axis_at), (blocks,), jnp.float32, low / len(shards), largest / len(shards)))
        level = level * jnp.repeat(draws, dims[axis_at] // blocks).reshape([-1 if axis == axis_at else 1 for axis in range(len(dims))])
    return level


def normal_values(rng, shape, scale, reach, split=(), kind=jnp.bfloat16):
    drawn = scale * jax.random.normal(rng, shape, jnp.float32)
    if split:
        drawn = drawn * steps_of(rng, shape, split, -0.22, 0.18)
    return jnp.clip(drawn, -reach, reach).astype(kind)


def setup_inputs(seed: int = 0) -> dict:
    streams_of = jax.random.split(jax.random.key(seed), 5)
    return {
        "tokens": normal_values(streams_of[0], (TOKENS, D), 1.0, 6.0, ((0, 4), (1, 8))),
        "gain": jnp.clip(1.0 + 0.18 * jax.random.normal(streams_of[1], (D,), jnp.float32), 0.1, 1.9),
        "proj": normal_values(streams_of[2], (D, D), D ** -0.5, 0.0625, ((0, 4), (1, 8))),
        "panel_index": jax.random.randint(streams_of[3], (1,), 0, D // PANEL).astype(jnp.int32),
    }


def reference(tokens, gain, proj, panel_index):
    values = tokens.astype(jnp.float32)
    inv_rms = lax.rsqrt(lax.optimization_barrier(jnp.mean(values * values, axis=1, keepdims=True)) + 1e-05)
    normed = (values * inv_rms * gain[None, :]).astype(jnp.bfloat16)
    outputs = (values + jnp.dot(normed.astype(jnp.float32), proj.astype(jnp.float32), preferred_element_type=jnp.float32)).astype(jnp.bfloat16)
    change = (outputs.astype(jnp.float32) - values).astype(jnp.bfloat16)
    band_start = panel_index[0].astype(jnp.int32) * PANEL
    band_cols = lax.dynamic_slice_in_dim(tokens, band_start, PANEL, 1)
    token_count = tokens.shape[0]
    gram_rows = jnp.dot(band_cols.T.astype(jnp.float32), tokens.astype(jnp.float32), preferred_element_type=jnp.float32) / token_count
    row_ids = lax.broadcasted_iota(jnp.int32, (PANEL, D), 0)
    col_ids = lax.broadcasted_iota(jnp.int32, (PANEL, D), 1)
    ridge_mask = jnp.where(col_ids == row_ids + band_start, 0.1, 0.0).astype(jnp.float32)
    gram_rows = gram_rows + ridge_mask
    cross_rows = jnp.dot(band_cols.T.astype(jnp.float32), change.astype(jnp.float32), preferred_element_type=jnp.float32) * (math.sqrt(D) / token_count)
    diag_block = lax.dynamic_slice_in_dim(gram_rows, band_start, PANEL, 1)
    factor = jnp.linalg.cholesky(diag_block)
    panel_rows = lax.linalg.triangular_solve(factor, gram_rows, left_side=True, lower=True)
    solved_cross = lax.linalg.triangular_solve(factor, cross_rows, left_side=True, lower=True)
    return (panel_rows, solved_cross)
```

```python
import math

import jax
import jax.numpy as jnp
from jax import lax
from jax.experimental import pallas as pl
from jax.experimental.pallas import tpu as pltpu
from jax.sharding import PartitionSpec as P

D = 8192
PANEL = 256
MESH = pl.DeviceIdType.MESH
HIGH = lax.Precision.HIGHEST
F32 = jnp.float32
BF16 = jnp.bfloat16
STEP = 32
TILE = 128
OUTER = PANEL // STEP
REST = PANEL - STEP


def dot0(a, b, precision=None):
    return lax.dot_general(a, b, (((0,), (0,)), ((), ())), precision=precision, preferred_element_type=F32)


def lanes(col):
    return jnp.broadcast_to(col, (8, TILE))


def eliminate(ob, wa, wi):
    r0 = pl.multiple_of(ob * STEP, STEP)
    groups = []
    for g in range(STEP // 8):
        rows = pl.ds(pl.multiple_of(r0 + 8 * g, 8), 8)
        groups.append(
            [wa[rows, 0:128], wa[rows, 128:256], wi[rows, 0:128], wi[rows, 128:256]]
        )
    sub = lax.broadcasted_iota(jnp.int32, (8, TILE), 0)
    n = STEP // 8
    for k in range(n):
        cols = {
            g: [lanes(groups[g][0][:, 8 * k + j : 8 * k + j + 1]) for j in range(8)]
            for g in range(k, n)
        }
        a = [[lanes(cols[k][j][i : i + 1, :]) if j <= i else None for j in range(8)] for i in range(8)]
        low = [[None] * 8 for _ in range(8)]
        inv = [None] * 8
        for j in range(8):
            inv[j] = lax.rsqrt(a[j][j])
            for i in range(j + 1, 8):
                low[i][j] = a[i][j] * inv[j]
            for l in range(j + 1, 8):
                for i in range(l, 8):
                    a[i][l] = a[i][l] - low[i][j] * low[l][j]
        m = [[None] * 8 for _ in range(8)]
        for j in range(8):
            m[j][j] = inv[j]
            for i in range(j + 1, 8):
                acc = low[i][j] * m[j][j]
                for l in range(j + 1, i):
                    acc = acc + low[i][l] * m[l][j]
                m[i][j] = -inv[i] * acc
        zero = jnp.zeros((8, TILE), F32)
        mcol, mrow = [], []
        for j in range(8):
            c = zero
            for i in range(j, 8):
                c = jnp.where(sub == i, m[i][j], c)
            mcol.append(c)
        for i in range(8):
            c = zero
            for j in range(0, i + 1):
                c = jnp.where(sub == j, m[i][j], c)
            mrow.append(c)
        done = []
        for v in range(4):
            r = groups[k][v]
            u = mcol[0] * lanes(r[0:1, :])
            for j in range(1, 8):
                u = u + mcol[j] * lanes(r[j : j + 1, :])
            done.append(u)
            if k < n - 1:
                w = mrow[0] * lanes(u[0:1, :])
                for j in range(1, 8):
                    w = w + mrow[j] * lanes(u[j : j + 1, :])
                wb = [lanes(w[j : j + 1, :]) for j in range(8)]
                for g in range(k + 1, n):
                    s = cols[g][0] * wb[0]
                    for j in range(1, 8):
                        s = s + cols[g][j] * wb[j]
                    groups[g][v] = groups[g][v] - s
        groups[k] = done
    for g in range(n):
        rows = pl.ds(pl.multiple_of(r0 + 8 * g, 8), 8)
        wi[rows, 0:128] = groups[g][2]
        wi[rows, 128:256] = groups[g][3]
    ua = jnp.concatenate(
        [jnp.concatenate([groups[g][0] for g in range(n)], axis=0), jnp.concatenate([groups[g][1] for g in range(n)], axis=0)],
        axis=1,
    )
    ui = jnp.concatenate(
        [jnp.concatenate([groups[g][2] for g in range(n)], axis=0), jnp.concatenate([groups[g][3] for g in range(n)], axis=0)],
        axis=1,
    )
    rest = pl.ds(pl.multiple_of(r0 + STEP, STEP), REST)
    left = ua[:, STEP:]
    if STEP % 128:
        left = pltpu.roll(ua, PANEL - STEP, 1)
    wa[rest, :] = pltpu.roll(wa[rest, :] - dot0(left, ua, HIGH)[:REST], PANEL - STEP, 1)
    wi[rest, :] = wi[rest, :] - dot0(left, ui, HIGH)[:REST]


def kernel(
    tcount, fcount, tokens, gain, proj_hbm, slice_ref, rel, panel, solved,
    proj, bfb, btb, own, zbuf, xbuf, xg, ssb, rsb, rss, agb, wa, wi, accs, inv_ref,
    proj_sem, bf_s, bf_r, bt_s, bt_r, oc_s, oc_r, a1_s, a1_r, a2_s, a2_r, a3_s, a3_r,
    ss_s, ss_r, rs_s, rs_r, ag_s, ag_r,
):
    t = lax.axis_index("tok")
    f = lax.axis_index("feat")
    z, c = f // 2, f % 2
    sib = f + 1 - 2 * c
    zcount = fcount // 2
    rows, cols = tokens.shape
    total = rows * tcount
    quarter = cols // tcount

    load = pltpu.make_async_copy(proj_hbm, proj, proj_sem)
    load.start()
    barrier = pltpu.get_barrier_semaphore()
    for d in range(1, fcount):
        pl.semaphore_signal(barrier, inc=1, device_id=(t, (f + d) % fcount), device_id_type=MESH)
    for d in range(1, tcount):
        pl.semaphore_signal(barrier, inc=1, device_id=((t + d) % tcount, f), device_id_type=MESH)
    bfb[f] = slice_ref[...]
    own[t] = tokens[...]
    zbuf[z] = tokens[...]
    pl.semaphore_wait(barrier, fcount + tcount - 2)

    def to(src, dst, ssem, rsem, device):
        return pltpu.make_async_remote_copy(
            src_ref=src, dst_ref=dst, send_sem=ssem, recv_sem=rsem, device_id=device, device_id_type=MESH
        )

    sent = []

    def send(src, dst, ssem, rsem, device):
        copy = to(src, dst, ssem, rsem, device)
        copy.start()
        sent.append(copy)

    def got(buf, slot, rsem):
        to(buf.at[slot], buf.at[slot], rsem.at[slot], rsem.at[slot], (t, sib)).wait_recv()

    for d in range(1, fcount):
        send(bfb.at[f], bfb.at[f], bf_s.at[d], bf_r.at[f], (t, (f + d) % fcount))
    for d in range(1, tcount):
        send(own.at[t], own.at[t], oc_s.at[d], oc_r.at[t], ((t + d) % tcount, f))
    for d in range(1, zcount):
        send(zbuf.at[z], zbuf.at[z], a1_s.at[d], a1_r.at[z], (t, ((z + d) % zcount) * 2 + c))

    def pass_on(d):
        zz = (z + d) % zcount
        if d:
            got(zbuf, zz, a1_r)

        @pl.when(zz == t)
        def _():
            xbuf[c, t] = zbuf[zz]

        @pl.when(zz != t)
        def _():
            to(zbuf.at[zz], xbuf.at[c, t], a2_s.at[d], a2_r.at[t], (zz, f)).start()

    def pass_done(d):
        zz = (z + d) % zcount

        @pl.when(zz != t)
        def _():
            to(zbuf.at[zz], xbuf.at[c, t], a2_s.at[d], a2_r.at[t], (zz, f)).wait_send()

    pass_on(0)
    for d in range(1, fcount):
        got(bfb, (f + d) % fcount, bf_r)
    whole = bfb[0].astype(F32)
    for d in range(1, fcount):
        whole = whole + bfb[d].astype(F32)
    btb[t] = whole.astype(BF16)
    for d in range(1, tcount):
        send(btb.at[t], btb.at[t], bt_s.at[d], bt_r.at[t], ((t + d) % tcount, f))
    for d in range(1, tcount):
        got(btb, (t + d) % tcount, bt_r)
    band = btb[...].reshape(total, PANEL)
    eye = (
        lax.broadcasted_iota(jnp.int32, (PANEL, PANEL), 0) == lax.broadcasted_iota(jnp.int32, (PANEL, PANEL), 1)
    ).astype(F32)
    wa[0:PANEL, :] = dot0(band, band) / total + 0.1 * eye
    wi[0:PANEL, :] = eye
    wa[PANEL:, :] = jnp.zeros((PANEL, PANEL), F32)
    wi[PANEL:, :] = jnp.zeros((PANEL, PANEL), F32)

    def chol(lo, hi):
        @pl.loop(lo, hi)
        def _(ob):
            eliminate(ob, wa, wi)

    chol(0, 1)
    for d in range(1, tcount):
        got(own, (t + d) % tcount, oc_r)
    wide = own[...].reshape(total, cols).astype(F32)
    ssb[f] = lax.dot_general(
        jnp.ones((8, cols), F32), wide * wide, (((1,), (1,)), ((), ())), precision=HIGH, preferred_element_type=F32
    )
    for d in range(1, fcount):
        send(ssb.at[f], ssb.at[f], ss_s.at[d], ss_r.at[f], (t, (f + d) % fcount))
    chol(1, 3)
    pass_on(1)
    pass_on(3)
    chol(3, 4)
    pass_on(2)
    for d in range(1, fcount):
        got(ssb, (f + d) % fcount, ss_r)
    sums = ssb[0]
    for d in range(1, fcount):
        sums = sums + ssb[d]
    inv_row = lax.rsqrt(sums / (cols * fcount) + 1e-05)
    inv_ref[...] = dot0(inv_row, jnp.full((8, TILE), 0.125, F32), HIGH)
    chol(4, 6)

    def share(d):
        tt = (t + d) % tcount
        if d:
            to(xbuf.at[c, tt], xbuf.at[c, tt], a2_r.at[tt], a2_r.at[tt], (t, sib)).wait_recv()
        send(xbuf.at[c, tt], xbuf.at[c, tt], a3_s.at[d], a3_r.at[tt], (t, sib))

    for d in range(tcount):
        share(d)
    width = 2 * cols

    def scaled(half):
        g = gain[:, pl.ds(pl.multiple_of(t * width + half * cols, cols), cols)]
        xg[half] = (xbuf[half].reshape(total, cols).astype(F32) * g).astype(BF16)

    scaled(c)
    for d in range(tcount):
        tt = (t + d) % tcount
        to(xbuf.at[1 - c, tt], xbuf.at[1 - c, tt], a3_r.at[tt], a3_r.at[tt], (t, sib)).wait_recv()
    scaled(1 - c)
    load.wait()
    for d in list(range(1, tcount)) + [0]:
        q = (t + d) % tcount
        at = pl.ds(pl.multiple_of(q * quarter, quarter), quarter)
        part = jnp.dot(xg[0], proj[0:cols, at], preferred_element_type=F32)
        part = part + jnp.dot(xg[1], proj[cols : 2 * cols, at], preferred_element_type=F32)
        if d:
            rss[q] = part.astype(BF16)
            send(rss.at[q], rsb.at[t], rs_s.at[d], rs_r.at[t], (q, f))
        else:
            accs[...] = part
    chol(6, OUTER)
    linv = wi[0:PANEL, :]
    for d in range(1, tcount):
        got(rsb, (t + d) % tcount, rs_r)
    acc = accs[...]
    for d in range(1, tcount):
        acc = acc + rsb[(t + d) % tcount].astype(F32)
    inv2 = jnp.concatenate([inv_ref[...]] * (quarter // TILE), axis=1)
    mine = own[:, :, pl.ds(pl.multiple_of(t * quarter, quarter), quarter)].reshape(total, quarter).astype(F32)
    out = (mine + acc * inv2).astype(BF16)
    change = (out.astype(F32) - mine).astype(BF16)
    band = btb[...].reshape(total, PANEL)
    cross = dot0(band, change) * (math.sqrt(D) / total)
    result = jnp.dot(linv, cross, precision=HIGH, preferred_element_type=F32)
    agb[t] = result.astype(BF16)
    for d in range(1, tcount):
        send(agb.at[t], agb.at[t], ag_s.at[d], ag_r.at[t], ((t + d) % tcount, f))
    shape = (PANEL, quarter)
    for q in range(tcount):
        at = slice(q * quarter, (q + 1) * quarter)
        gram = dot0(band, own[:, :, at].reshape(total, quarter)) / total
        row_ids = lax.broadcasted_iota(jnp.int32, shape, 0)
        col_ids = jnp.broadcast_to(rel[:, at], shape)
        gram = gram + jnp.where(col_ids == row_ids, 0.1, 0.0).astype(F32)
        panel[:, at] = jnp.dot(linv, gram, precision=HIGH, preferred_element_type=F32)
    solved[:, pl.ds(pl.multiple_of(t * quarter, quarter), quarter)] = result
    for d in range(1, tcount):
        q = (t + d) % tcount
        got(agb, q, ag_r)
        solved[:, pl.ds(pl.multiple_of(q * quarter, quarter), quarter)] = agb[q].astype(F32)
    for copy in sent:
        copy.wait_send()
    for d in range(zcount):
        pass_done(d)


def fused(tcount, fcount, tokens, gain, proj, panel_index):
    rows, cols = tokens.shape
    total, quarter, zcount = rows * tcount, cols // tcount, fcount // 2
    start = panel_index[0] * PANEL
    f = lax.axis_index("feat")
    band_slice = lax.dynamic_slice_in_dim(tokens, start % cols, PANEL, 1)
    band_slice = jnp.where(start // cols == f, band_slice, jnp.zeros_like(band_slice))
    rel = (lax.broadcasted_iota(jnp.int32, (1, cols), 1) + (f * cols - start)).astype(jnp.int32)
    vmem = pl.BlockSpec(memory_space=pltpu.VMEM)
    dma = lambda n: pltpu.SemaphoreType.DMA((n,))
    scratch = [
        pltpu.VMEM(proj.shape, BF16),
        pltpu.VMEM((fcount, rows, PANEL), BF16),
        pltpu.VMEM((tcount, rows, PANEL), BF16),
        pltpu.VMEM((tcount, rows, cols), BF16),
        pltpu.VMEM((zcount, rows, cols), BF16),
        pltpu.VMEM((2, tcount, rows, cols), BF16),
        pltpu.VMEM((2, total, cols), BF16),
        pltpu.VMEM((fcount, 8, total), F32),
        pltpu.VMEM((tcount, total, quarter), BF16),
        pltpu.VMEM((tcount, total, quarter), BF16),
        pltpu.VMEM((tcount, PANEL, quarter), BF16),
        pltpu.VMEM((2 * PANEL, PANEL), F32),
        pltpu.VMEM((2 * PANEL, PANEL), F32),
        pltpu.VMEM((total, quarter), F32),
        pltpu.VMEM((total, TILE), F32),
        pltpu.SemaphoreType.DMA,
    ]
    for n in (fcount, tcount, tcount, zcount, tcount, tcount, fcount, tcount, tcount):
        scratch += [dma(n), dma(n)]
    out = jax.ShapeDtypeStruct((PANEL, cols), F32)
    return pl.pallas_call(
        lambda *refs: kernel(tcount, fcount, *refs),
        out_shape=(out, out),
        in_specs=[vmem, vmem, pl.BlockSpec(memory_space=pl.ANY), vmem, vmem],
        out_specs=(vmem, vmem),
        scratch_shapes=scratch,
        compiler_params=pltpu.CompilerParams(
            collective_id=0, has_side_effects=True, vmem_limit_bytes=48 * 1024 * 1024
        ),
    )(tokens, gain[None, :], proj, band_slice, rel)

def solve_pair(factor, gram_part, cross_part):
    first = lax.linalg.triangular_solve(factor, gram_part, left_side=True, lower=True)
    second = lax.linalg.triangular_solve(factor, cross_part, left_side=True, lower=True)
    return (first, second)


def general(tokens, gain, proj, panel_index):
    token_full = lax.all_gather(tokens, "feat", axis=1, tiled=True)
    wide_rows = token_full.astype(jnp.float32)
    inv_rms = lax.rsqrt(jnp.mean(wide_rows * wide_rows, axis=1, keepdims=True) + 1e-05)
    normed = (wide_rows * inv_rms * gain[None, :]).astype(jnp.bfloat16)
    local_cols = tokens.shape[1]
    projected = jnp.dot(
        normed, lax.all_gather(proj, "tok", axis=0, tiled=True), preferred_element_type=jnp.float32
    )
    own_values = tokens.astype(jnp.float32)
    outputs = (own_values + projected).astype(jnp.bfloat16)
    change = (outputs.astype(jnp.float32) - own_values).astype(jnp.bfloat16)
    band_start = panel_index[0] * PANEL
    band_cols = lax.dynamic_slice_in_dim(token_full, band_start, PANEL, 1)
    gram_part = jnp.dot(band_cols.T, tokens, preferred_element_type=jnp.float32)
    cross_part = jnp.dot(band_cols.T, change, preferred_element_type=jnp.float32)
    gram_sum, cross_sum = (
        lax.psum_scatter(gram_part, "tok", scatter_dimension=0, tiled=True),
        lax.psum_scatter(cross_part, "tok", scatter_dimension=0, tiled=True),
    )
    tok_count = lax.axis_size("tok")
    feat_count = lax.axis_size("feat")
    token_count = tokens.shape[0] * tok_count
    rows_here = gram_sum.shape[0]
    row_ids = lax.broadcasted_iota(jnp.int32, gram_sum.shape, 0) + lax.axis_index("tok") * rows_here
    col_ids = (
        lax.broadcasted_iota(jnp.int32, gram_sum.shape, 1) + lax.axis_index("feat") * local_cols
    )
    ridge_mask = jnp.where(col_ids == row_ids + band_start, 0.1, 0.0).astype(jnp.float32)
    gram_rows = gram_sum / token_count + ridge_mask
    cross_rows = cross_sum * (math.sqrt(D) / token_count)
    slab_rows = PANEL // feat_count
    own_slab = lax.dynamic_slice_in_dim(band_cols, lax.axis_index("feat") * slab_rows, slab_rows, 1)
    partial_value = jnp.dot(own_slab.T, band_cols, preferred_element_type=jnp.float32)
    summed = lax.psum(partial_value, "tok")
    diag_sum = lax.all_gather(summed, "feat", axis=0, tiled=True)
    diag_block = diag_sum / token_count + 0.1 * jnp.eye(PANEL, dtype=jnp.float32)
    factor = jnp.linalg.cholesky(diag_block)
    gram_some, cross_some = (
        lax.all_to_all(gram_rows, "tok", split_axis=1, concat_axis=0, tiled=True),
        lax.all_to_all(cross_rows, "tok", split_axis=1, concat_axis=0, tiled=True),
    )
    panel_some, solved_some = solve_pair(factor, gram_some, cross_some)
    panel_rows, solved_cross = (
        lax.all_gather(panel_some, "tok", axis=1, tiled=True),
        lax.all_gather(solved_some, "tok", axis=1, tiled=True),
    )
    return (panel_rows, solved_cross)


def solution(mesh):
    tcount, fcount = mesh.shape["tok"], mesh.shape["feat"]

    def body(tokens, gain, proj, panel_index):
        rows, cols = tokens.shape
        fits = (
            fcount == 2 * tcount
            and proj.shape[0] == 2 * cols
            and rows % 16 == 0
            and rows * tcount == PANEL
            and cols % (tcount * TILE) == 0
            and cols % PANEL == 0
        )
        if fits:
            return fused(tcount, fcount, tokens, gain, proj, panel_index)
        return general(tokens, gain, proj, panel_index)

    return jax.shard_map(
        body,
        mesh=mesh,
        in_specs=(P("tok", "feat"), P(), P("tok", "feat"), P()),
        out_specs=(P(None, "feat"), P(None, "feat")),
        check_vma=False,
    )
```

```python
import math

import jax
import jax.numpy as jnp
from jax import lax
from jax.experimental import pallas as pl
from jax.experimental.pallas import tpu as pltpu
from jax.sharding import PartitionSpec as P

D = 8192
PANEL = 256
MESH = pl.DeviceIdType.MESH
HIGH = lax.Precision.HIGHEST
F32 = jnp.float32
BF16 = jnp.bfloat16
STEP = 32
TILE = 128
OUTER = PANEL // STEP
REST = PANEL - STEP


def dot0(a, b, precision=None):
    return lax.dot_general(a, b, (((0,), (0,)), ((), ())), precision=precision, preferred_element_type=F32)


def lanes(col):
    return jnp.broadcast_to(col, (8, TILE))


def eliminate(ob, wa, wi):
    r0 = pl.multiple_of(ob * STEP, STEP)
    groups = []
    for g in range(STEP // 8):
        rows = pl.ds(pl.multiple_of(r0 + 8 * g, 8), 8)
        groups.append(
            [wa[rows, 0:128], wa[rows, 128:256], wi[rows, 0:128], wi[rows, 128:256]]
        )
    sub = lax.broadcasted_iota(jnp.int32, (8, TILE), 0)
    n = STEP // 8
    for k in range(n):
        cols = {
            g: [lanes(groups[g][0][:, 8 * k + j : 8 * k + j + 1]) for j in range(8)]
            for g in range(k, n)
        }
        a = [[lanes(cols[k][j][i : i + 1, :]) if j <= i else None for j in range(8)] for i in range(8)]
        low = [[None] * 8 for _ in range(8)]
        inv = [None] * 8
        for j in range(8):
            inv[j] = lax.rsqrt(a[j][j])
            for i in range(j + 1, 8):
                low[i][j] = a[i][j] * inv[j]
            for l in range(j + 1, 8):
                for i in range(l, 8):
                    a[i][l] = a[i][l] - low[i][j] * low[l][j]
        m = [[None] * 8 for _ in range(8)]
        for j in range(8):
            m[j][j] = inv[j]
            for i in range(j + 1, 8):
                acc = low[i][j] * m[j][j]
                for l in range(j + 1, i):
                    acc = acc + low[i][l] * m[l][j]
                m[i][j] = -inv[i] * acc
        zero = jnp.zeros((8, TILE), F32)
        mcol, mrow = [], []
        for j in range(8):
            c = zero
            for i in range(j, 8):
                c = jnp.where(sub == i, m[i][j], c)
            mcol.append(c)
        for i in range(8):
            c = zero
            for j in range(0, i + 1):
                c = jnp.where(sub == j, m[i][j], c)
            mrow.append(c)
        done = []
        for v in range(4):
            r = groups[k][v]
            u = mcol[0] * lanes(r[0:1, :])
            for j in range(1, 8):
                u = u + mcol[j] * lanes(r[j : j + 1, :])
            done.append(u)
            if k < n - 1:
                w = mrow[0] * lanes(u[0:1, :])
                for j in range(1, 8):
                    w = w + mrow[j] * lanes(u[j : j + 1, :])
                wb = [lanes(w[j : j + 1, :]) for j in range(8)]
                for g in range(k + 1, n):
                    s = cols[g][0] * wb[0]
                    for j in range(1, 8):
                        s = s + cols[g][j] * wb[j]
                    groups[g][v] = groups[g][v] - s
        groups[k] = done
    for g in range(n):
        rows = pl.ds(pl.multiple_of(r0 + 8 * g, 8), 8)
        wi[rows, 0:128] = groups[g][2]
        wi[rows, 128:256] = groups[g][3]
    ua = jnp.concatenate(
        [jnp.concatenate([groups[g][0] for g in range(n)], axis=0), jnp.concatenate([groups[g][1] for g in range(n)], axis=0)],
        axis=1,
    )
    ui = jnp.concatenate(
        [jnp.concatenate([groups[g][2] for g in range(n)], axis=0), jnp.concatenate([groups[g][3] for g in range(n)], axis=0)],
        axis=1,
    )
    rest = pl.ds(pl.multiple_of(r0 + STEP, STEP), REST)
    left = ua[:, STEP:]
    if STEP % 128:
        left = pltpu.roll(ua, PANEL - STEP, 1)
    wa[rest, :] = pltpu.roll(wa[rest, :] - dot0(left, ua, HIGH)[:REST], PANEL - STEP, 1)
    wi[rest, :] = wi[rest, :] - dot0(left, ui, HIGH)[:REST]


def kernel(
    tcount, fcount, tokens, gain_hbm, proj_hbm, pidx, panel, solved,
    proj, gain, bfb, btb, own, zbuf, xbuf, xg, ssb, rsb, rss, agb, wa, wi, accs, inv_ref,
    proj_sem, gain_sem, own_sem, z_sem, bf_s, bf_r, bt_s, bt_r, oc_s, oc_r, a1_s, a1_r, a2_s, a2_r, a3_s, a3_r,
    ss_s, ss_r, rs_s, rs_r, ag_s, ag_r,
):
    t = lax.axis_index("tok")
    f = lax.axis_index("feat")
    z, c = f // 2, f % 2
    sib = f + 1 - 2 * c
    zcount = fcount // 2
    rows, cols = tokens.shape
    total = rows * tcount
    quarter = cols // tcount

    load = pltpu.make_async_copy(proj_hbm, proj, proj_sem)
    start = pidx[0] * PANEL
    load_own = pltpu.make_async_copy(tokens, own.at[t], own_sem)
    load_own.start()
    load_z = pltpu.make_async_copy(tokens, zbuf.at[z], z_sem)
    load_z.start()
    load_gain = pltpu.make_async_copy(gain_hbm, gain, gain_sem)
    load_gain.start()
    load.start()
    barrier = pltpu.get_barrier_semaphore()
    for d in range(1, fcount):
        pl.semaphore_signal(barrier, inc=1, device_id=(t, (f + d) % fcount), device_id_type=MESH)
    for d in range(1, tcount):
        pl.semaphore_signal(barrier, inc=1, device_id=((t + d) % tcount, f), device_id_type=MESH)
    shape = (cols, PANEL)
    pick = lax.broadcasted_iota(jnp.int32, shape, 0) + f * cols == lax.broadcasted_iota(jnp.int32, shape, 1) + start
    pick = jnp.where(pick, 1.0, 0.0).astype(BF16)
    load_own.wait()
    bfb[f] = jnp.dot(own[t], pick, preferred_element_type=F32).astype(BF16)
    load_z.wait()
    pl.semaphore_wait(barrier, fcount + tcount - 2)

    def to(src, dst, ssem, rsem, device):
        return pltpu.make_async_remote_copy(
            src_ref=src, dst_ref=dst, send_sem=ssem, recv_sem=rsem, device_id=device, device_id_type=MESH
        )

    sent = []

    def send(src, dst, ssem, rsem, device):
        copy = to(src, dst, ssem, rsem, device)
        copy.start()
        sent.append(copy)

    def got(buf, slot, rsem):
        to(buf.at[slot], buf.at[slot], rsem.at[slot], rsem.at[slot], (t, sib)).wait_recv()

    for d in range(1, fcount):
        send(bfb.at[f], bfb.at[f], bf_s.at[d], bf_r.at[f], (t, (f + d) % fcount))
    for d in range(1, tcount):
        send(own.at[t], own.at[t], oc_s.at[d], oc_r.at[t], ((t + d) % tcount, f))
    for d in range(1, zcount):
        send(zbuf.at[z], zbuf.at[z], a1_s.at[d], a1_r.at[z], (t, ((z + d) % zcount) * 2 + c))

    def pass_on(d):
        zz = (z + d) % zcount
        if d:
            got(zbuf, zz, a1_r)

        @pl.when(zz == t)
        def _():
            xbuf[c, t] = zbuf[zz]

        @pl.when(zz != t)
        def _():
            to(zbuf.at[zz], xbuf.at[c, t], a2_s.at[d], a2_r.at[t], (zz, f)).start()

    def pass_done(d):
        zz = (z + d) % zcount

        @pl.when(zz != t)
        def _():
            to(zbuf.at[zz], xbuf.at[c, t], a2_s.at[d], a2_r.at[t], (zz, f)).wait_send()

    pass_on(0)
    def share(d):
        tt = (t + d) % tcount
        if d:
            to(xbuf.at[c, tt], xbuf.at[c, tt], a2_r.at[tt], a2_r.at[tt], (t, sib)).wait_recv()
        send(xbuf.at[c, tt], xbuf.at[c, tt], a3_s.at[d], a3_r.at[tt], (t, sib))

    for d in range(1, fcount):
        got(bfb, (f + d) % fcount, bf_r)
    whole = bfb[0].astype(F32)
    for d in range(1, fcount):
        whole = whole + bfb[d].astype(F32)
    btb[t] = whole.astype(BF16)
    for d in range(1, tcount):
        send(btb.at[t], btb.at[t], bt_s.at[d], bt_r.at[t], ((t + d) % tcount, f))
    pass_on(1)
    pass_on(3)
    for d in range(1, tcount):
        got(btb, (t + d) % tcount, bt_r)
    band = btb[...].reshape(total, PANEL)
    eye = (
        lax.broadcasted_iota(jnp.int32, (PANEL, PANEL), 0) == lax.broadcasted_iota(jnp.int32, (PANEL, PANEL), 1)
    ).astype(F32)
    wa[0:PANEL, :] = dot0(band, band) / total + 0.1 * eye
    wi[0:PANEL, :] = eye
    wa[PANEL:, :] = jnp.zeros((PANEL, PANEL), F32)
    wi[PANEL:, :] = jnp.zeros((PANEL, PANEL), F32)

    def chol(lo, hi):
        @pl.loop(lo, hi)
        def _(ob):
            eliminate(ob, wa, wi)

    chol(0, 1)
    pass_on(2)
    for d in range(1, tcount):
        got(own, (t + d) % tcount, oc_r)
    wide = own[...].reshape(total, cols).astype(F32)
    wide = wide * wide
    fold = wide[:, 0:TILE]
    for v in range(1, cols // TILE):
        fold = fold + wide[:, v * TILE : (v + 1) * TILE]
    ssb[f] = lax.dot_general(
        jnp.ones((8, TILE), F32), fold, (((1,), (1,)), ((), ())), precision=HIGH, preferred_element_type=F32
    )
    for d in range(1, fcount):
        send(ssb.at[f], ssb.at[f], ss_s.at[d], ss_r.at[f], (t, (f + d) % fcount))
    chol(1, 3)
    share(0)
    share(1)
    share(3)
    share(2)

    width = 2 * cols

    def scaled(half):
        g = gain[:, pl.ds(pl.multiple_of(t * width + half * cols, cols), cols)]
        xg[half] = (xbuf[half].reshape(total, cols).astype(F32) * g).astype(BF16)

    load_gain.wait()
    scaled(c)
    for d in range(tcount):
        tt = (t + d) % tcount
        to(xbuf.at[1 - c, tt], xbuf.at[1 - c, tt], a3_r.at[tt], a3_r.at[tt], (t, sib)).wait_recv()
    scaled(1 - c)
    load.wait()
    for d in list(range(1, tcount)) + [0]:
        q = (t + d) % tcount
        at = pl.ds(pl.multiple_of(q * quarter, quarter), quarter)
        part = jnp.dot(xg[0], proj[0:cols, at], preferred_element_type=F32)
        part = part + jnp.dot(xg[1], proj[cols : 2 * cols, at], preferred_element_type=F32)
        if d:
            rss[q] = part.astype(BF16)
            send(rss.at[q], rsb.at[t], rs_s.at[d], rs_r.at[t], (q, f))
        else:
            accs[...] = part
    for d in range(1, fcount):
        got(ssb, (f + d) % fcount, ss_r)
    sums = ssb[0]
    for d in range(1, fcount):
        sums = sums + ssb[d]
    inv_row = lax.rsqrt(sums / (cols * fcount) + 1e-05)
    inv_ref[...] = dot0(inv_row, jnp.full((8, TILE), 0.125, F32), HIGH)
    chol(3, OUTER)
    linv = wi[0:PANEL, :]
    for d in range(1, tcount):
        got(rsb, (t + d) % tcount, rs_r)
    acc = accs[...]
    for d in range(1, tcount):
        acc = acc + rsb[(t + d) % tcount].astype(F32)
    inv2 = jnp.concatenate([inv_ref[...]] * (quarter // TILE), axis=1)
    mine = own[:, :, pl.ds(pl.multiple_of(t * quarter, quarter), quarter)].reshape(total, quarter).astype(F32)
    out = (mine + acc * inv2).astype(BF16)
    change = (out.astype(F32) - mine).astype(BF16)
    band = btb[...].reshape(total, PANEL)
    cross = dot0(band, change) * (math.sqrt(D) / total)
    result = jnp.dot(linv, cross, precision=HIGH, preferred_element_type=F32)
    agb[t] = result.astype(BF16)
    for d in range(1, tcount):
        send(agb.at[t], agb.at[t], ag_s.at[d], ag_r.at[t], ((t + d) % tcount, f))
    shape = (PANEL, quarter)
    for q in range(tcount):
        at = slice(q * quarter, (q + 1) * quarter)
        gram = dot0(band, own[:, :, at].reshape(total, quarter)) / total
        row_ids = lax.broadcasted_iota(jnp.int32, shape, 0)
        col_ids = lax.broadcasted_iota(jnp.int32, shape, 1) + (f * cols + q * quarter)
        gram = gram + jnp.where(col_ids == row_ids + start, 0.1, 0.0).astype(F32)
        panel[:, at] = jnp.dot(linv, gram, precision=HIGH, preferred_element_type=F32)
    solved[:, pl.ds(pl.multiple_of(t * quarter, quarter), quarter)] = result
    for d in range(1, tcount):
        q = (t + d) % tcount
        got(agb, q, ag_r)
        solved[:, pl.ds(pl.multiple_of(q * quarter, quarter), quarter)] = agb[q].astype(F32)
    for copy in sent:
        copy.wait_send()
    for d in range(zcount):
        pass_done(d)


def fused(tcount, fcount, tokens, gain, proj, panel_index):
    rows, cols = tokens.shape
    total, quarter, zcount = rows * tcount, cols // tcount, fcount // 2
    vmem = pl.BlockSpec(memory_space=pltpu.VMEM)
    dma = lambda n: pltpu.SemaphoreType.DMA((n,))
    scratch = [
        pltpu.VMEM(proj.shape, BF16),
        pltpu.VMEM((1, gain.shape[0]), F32),
        pltpu.VMEM((fcount, rows, PANEL), BF16),
        pltpu.VMEM((tcount, rows, PANEL), BF16),
        pltpu.VMEM((tcount, rows, cols), BF16),
        pltpu.VMEM((zcount, rows, cols), BF16),
        pltpu.VMEM((2, tcount, rows, cols), BF16),
        pltpu.VMEM((2, total, cols), BF16),
        pltpu.VMEM((fcount, 8, total), F32),
        pltpu.VMEM((tcount, total, quarter), BF16),
        pltpu.VMEM((tcount, total, quarter), BF16),
        pltpu.VMEM((tcount, PANEL, quarter), BF16),
        pltpu.VMEM((2 * PANEL, PANEL), F32),
        pltpu.VMEM((2 * PANEL, PANEL), F32),
        pltpu.VMEM((total, quarter), F32),
        pltpu.VMEM((total, TILE), F32),
        pltpu.SemaphoreType.DMA,
        pltpu.SemaphoreType.DMA,
        pltpu.SemaphoreType.DMA,
        pltpu.SemaphoreType.DMA,
    ]
    for n in (fcount, tcount, tcount, zcount, tcount, tcount, fcount, tcount, tcount):
        scratch += [dma(n), dma(n)]
    out = jax.ShapeDtypeStruct((PANEL, cols), F32)
    return pl.pallas_call(
        lambda *refs: kernel(tcount, fcount, *refs),
        out_shape=(out, out),
        in_specs=[pl.BlockSpec(memory_space=pl.ANY)] * 3 + [pl.BlockSpec(memory_space=pltpu.SMEM)],
        out_specs=(vmem, vmem),
        scratch_shapes=scratch,
        compiler_params=pltpu.CompilerParams(
            collective_id=0, has_side_effects=True, vmem_limit_bytes=48 * 1024 * 1024
        ),
    )(tokens, gain[None, :], proj, panel_index)

def solve_pair(factor, gram_part, cross_part):
    first = lax.linalg.triangular_solve(factor, gram_part, left_side=True, lower=True)
    second = lax.linalg.triangular_solve(factor, cross_part, left_side=True, lower=True)
    return (first, second)


def general(tokens, gain, proj, panel_index):
    token_full = lax.all_gather(tokens, "feat", axis=1, tiled=True)
    wide_rows = token_full.astype(jnp.float32)
    inv_rms = lax.rsqrt(jnp.mean(wide_rows * wide_rows, axis=1, keepdims=True) + 1e-05)
    normed = (wide_rows * inv_rms * gain[None, :]).astype(jnp.bfloat16)
    local_cols = tokens.shape[1]
    projected = jnp.dot(
        normed, lax.all_gather(proj, "tok", axis=0, tiled=True), preferred_element_type=jnp.float32
    )
    own_values = tokens.astype(jnp.float32)
    outputs = (own_values + projected).astype(jnp.bfloat16)
    change = (outputs.astype(jnp.float32) - own_values).astype(jnp.bfloat16)
    band_start = panel_index[0] * PANEL
    band_cols = lax.dynamic_slice_in_dim(token_full, band_start, PANEL, 1)
    gram_part = jnp.dot(band_cols.T, tokens, preferred_element_type=jnp.float32)
    cross_part = jnp.dot(band_cols.T, change, preferred_element_type=jnp.float32)
    gram_sum, cross_sum = (
        lax.psum_scatter(gram_part, "tok", scatter_dimension=0, tiled=True),
        lax.psum_scatter(cross_part, "tok", scatter_dimension=0, tiled=True),
    )
    tok_count = lax.axis_size("tok")
    feat_count = lax.axis_size("feat")
    token_count = tokens.shape[0] * tok_count
    rows_here = gram_sum.shape[0]
    row_ids = lax.broadcasted_iota(jnp.int32, gram_sum.shape, 0) + lax.axis_index("tok") * rows_here
    col_ids = (
        lax.broadcasted_iota(jnp.int32, gram_sum.shape, 1) + lax.axis_index("feat") * local_cols
    )
    ridge_mask = jnp.where(col_ids == row_ids + band_start, 0.1, 0.0).astype(jnp.float32)
    gram_rows = gram_sum / token_count + ridge_mask
    cross_rows = cross_sum * (math.sqrt(D) / token_count)
    slab_rows = PANEL // feat_count
    own_slab = lax.dynamic_slice_in_dim(band_cols, lax.axis_index("feat") * slab_rows, slab_rows, 1)
    partial_value = jnp.dot(own_slab.T, band_cols, preferred_element_type=jnp.float32)
    summed = lax.psum(partial_value, "tok")
    diag_sum = lax.all_gather(summed, "feat", axis=0, tiled=True)
    diag_block = diag_sum / token_count + 0.1 * jnp.eye(PANEL, dtype=jnp.float32)
    factor = jnp.linalg.cholesky(diag_block)
    gram_some, cross_some = (
        lax.all_to_all(gram_rows, "tok", split_axis=1, concat_axis=0, tiled=True),
        lax.all_to_all(cross_rows, "tok", split_axis=1, concat_axis=0, tiled=True),
    )
    panel_some, solved_some = solve_pair(factor, gram_some, cross_some)
    panel_rows, solved_cross = (
        lax.all_gather(panel_some, "tok", axis=1, tiled=True),
        lax.all_gather(solved_some, "tok", axis=1, tiled=True),
    )
    return (panel_rows, solved_cross)


def solution(mesh):
    tcount, fcount = mesh.shape["tok"], mesh.shape["feat"]

    def body(tokens, gain, proj, panel_index):
        rows, cols = tokens.shape
        fits = (
            fcount == 2 * tcount
            and proj.shape[0] == 2 * cols
            and rows % 16 == 0
            and rows * tcount == PANEL
            and cols % (tcount * TILE) == 0
            and cols % PANEL == 0
        )
        if fits:
            return fused(tcount, fcount, tokens, gain, proj, panel_index)
        return general(tokens, gain, proj, panel_index)

    return jax.shard_map(
        body,
        mesh=mesh,
        in_specs=(P("tok", "feat"), P(), P("tok", "feat"), P()),
        out_specs=(P(None, "feat"), P(None, "feat")),
        check_vma=False,
    )
```

```python
import math

import jax
import jax.numpy as jnp
from jax import lax
from jax.experimental import pallas as pl
from jax.experimental.pallas import tpu as pltpu
from jax.sharding import PartitionSpec as P

D = 8192
PANEL = 256
MESH = pl.DeviceIdType.MESH
HIGH = lax.Precision.HIGHEST
F32 = jnp.float32
BF16 = jnp.bfloat16
STEP = 32
TILE = 128
OUTER = PANEL // STEP
REST = PANEL - STEP


def dot0(a, b, precision=None):
    return lax.dot_general(a, b, (((0,), (0,)), ((), ())), precision=precision, preferred_element_type=F32)


def lanes(col):
    return jnp.broadcast_to(col, (8, TILE))


def eliminate(ob, wa, wi):
    r0 = pl.multiple_of(ob * STEP, STEP)
    groups = []
    for g in range(STEP // 8):
        rows = pl.ds(pl.multiple_of(r0 + 8 * g, 8), 8)
        groups.append(
            [wa[rows, 0:128], wa[rows, 128:256], wi[rows, 0:128], wi[rows, 128:256]]
        )
    sub = lax.broadcasted_iota(jnp.int32, (8, TILE), 0)
    n = STEP // 8
    for k in range(n):
        cols = {
            g: [lanes(groups[g][0][:, 8 * k + j : 8 * k + j + 1]) for j in range(8)]
            for g in range(k, n)
        }
        a = [[lanes(cols[k][j][i : i + 1, :]) if j <= i else None for j in range(8)] for i in range(8)]
        low = [[None] * 8 for _ in range(8)]
        inv = [None] * 8
        for j in range(8):
            inv[j] = lax.rsqrt(a[j][j])
            for i in range(j + 1, 8):
                low[i][j] = a[i][j] * inv[j]
            for l in range(j + 1, 8):
                for i in range(l, 8):
                    a[i][l] = a[i][l] - low[i][j] * low[l][j]
        m = [[None] * 8 for _ in range(8)]
        for j in range(8):
            m[j][j] = inv[j]
            for i in range(j + 1, 8):
                acc = low[i][j] * m[j][j]
                for l in range(j + 1, i):
                    acc = acc + low[i][l] * m[l][j]
                m[i][j] = -inv[i] * acc
        zero = jnp.zeros((8, TILE), F32)
        mcol, mrow = [], []
        for j in range(8):
            c = zero
            for i in range(j, 8):
                c = jnp.where(sub == i, m[i][j], c)
            mcol.append(c)
        for i in range(8):
            c = zero
            for j in range(0, i + 1):
                c = jnp.where(sub == j, m[i][j], c)
            mrow.append(c)
        done = []
        for v in range(4):
            r = groups[k][v]
            u = mcol[0] * lanes(r[0:1, :])
            for j in range(1, 8):
                u = u + mcol[j] * lanes(r[j : j + 1, :])
            done.append(u)
            if k < n - 1:
                w = mrow[0] * lanes(u[0:1, :])
                for j in range(1, 8):
                    w = w + mrow[j] * lanes(u[j : j + 1, :])
                wb = [lanes(w[j : j + 1, :]) for j in range(8)]
                for g in range(k + 1, n):
                    s = cols[g][0] * wb[0]
                    for j in range(1, 8):
                        s = s + cols[g][j] * wb[j]
                    groups[g][v] = groups[g][v] - s
        groups[k] = done
    for g in range(n):
        rows = pl.ds(pl.multiple_of(r0 + 8 * g, 8), 8)
        wi[rows, 0:128] = groups[g][2]
        wi[rows, 128:256] = groups[g][3]
    ua = jnp.concatenate(
        [jnp.concatenate([groups[g][0] for g in range(n)], axis=0), jnp.concatenate([groups[g][1] for g in range(n)], axis=0)],
        axis=1,
    )
    ui = jnp.concatenate(
        [jnp.concatenate([groups[g][2] for g in range(n)], axis=0), jnp.concatenate([groups[g][3] for g in range(n)], axis=0)],
        axis=1,
    )
    rest = pl.ds(pl.multiple_of(r0 + STEP, STEP), REST)
    left = ua[:, STEP:]
    if STEP % 128:
        left = pltpu.roll(ua, PANEL - STEP, 1)
    wa[rest, :] = pltpu.roll(wa[rest, :] - dot0(left, ua, HIGH)[:REST], PANEL - STEP, 1)
    wi[rest, :] = wi[rest, :] - dot0(left, ui, HIGH)[:REST]


def kernel(
    tcount, fcount, tokens, gain_hbm, proj_hbm, pidx, panel, solved,
    proj, gain, bfb, btb, own, zbuf, xbuf, xg, ssb, rsb, rss, agb, wa, wi, accs, inv_ref,
    proj_sem, gain_sem, own_sem, z_sem, bf_s, bf_r, bt_s, bt_r, oc_s, oc_r, a1_s, a1_r, a2_s, a2_r, a3_s, a3_r,
    ss_s, ss_r, rs_s, rs_r, ag_s, ag_r,
):
    t = lax.axis_index("tok")
    f = lax.axis_index("feat")
    z, c = f // 2, f % 2
    sib = f + 1 - 2 * c
    zcount = fcount // 2
    rows, cols = tokens.shape
    total = rows * tcount
    quarter = cols // tcount

    load = pltpu.make_async_copy(proj_hbm, proj, proj_sem)
    start = pidx[0] * PANEL
    load_own = pltpu.make_async_copy(tokens, own.at[t], own_sem)
    load_own.start()
    load_z = pltpu.make_async_copy(tokens, zbuf.at[z], z_sem)
    load_z.start()
    load_gain = pltpu.make_async_copy(gain_hbm, gain, gain_sem)
    load_gain.start()
    load.start()
    barrier = pltpu.get_barrier_semaphore()
    for d in range(1, fcount):
        pl.semaphore_signal(barrier, inc=1, device_id=(t, (f + d) % fcount), device_id_type=MESH)
    for d in range(1, tcount):
        pl.semaphore_signal(barrier, inc=1, device_id=((t + d) % tcount, f), device_id_type=MESH)
    shape = (cols, PANEL)
    pick = lax.broadcasted_iota(jnp.int32, shape, 0) + f * cols == lax.broadcasted_iota(jnp.int32, shape, 1) + start
    pick = jnp.where(pick, 1.0, 0.0).astype(BF16)
    load_own.wait()
    bfb[f] = jnp.dot(own[t], pick, preferred_element_type=F32).astype(BF16)
    load_z.wait()
    pl.semaphore_wait(barrier, fcount + tcount - 2)

    def to(src, dst, ssem, rsem, device):
        return pltpu.make_async_remote_copy(
            src_ref=src, dst_ref=dst, send_sem=ssem, recv_sem=rsem, device_id=device, device_id_type=MESH
        )

    sent = []

    def send(src, dst, ssem, rsem, device):
        copy = to(src, dst, ssem, rsem, device)
        copy.start()
        sent.append(copy)

    def got(buf, slot, rsem):
        to(buf.at[slot], buf.at[slot], rsem.at[slot], rsem.at[slot], (t, sib)).wait_recv()

    for d in range(1, fcount):
        send(bfb.at[f], bfb.at[f], bf_s.at[d], bf_r.at[f], (t, (f + d) % fcount))
    for d in range(1, tcount):
        send(own.at[t], own.at[t], oc_s.at[d], oc_r.at[t], ((t + d) % tcount, f))
    for d in range(1, zcount):
        send(zbuf.at[z], zbuf.at[z], a1_s.at[d], a1_r.at[z], (t, ((z + d) % zcount) * 2 + c))

    def pass_on(d):
        zz = (z + d) % zcount
        if d:
            got(zbuf, zz, a1_r)

        @pl.when(zz == t)
        def _():
            xbuf[c, t] = zbuf[zz]

        @pl.when(zz != t)
        def _():
            to(zbuf.at[zz], xbuf.at[c, t], a2_s.at[d], a2_r.at[t], (zz, f)).start()

    def pass_done(d):
        zz = (z + d) % zcount

        @pl.when(zz != t)
        def _():
            to(zbuf.at[zz], xbuf.at[c, t], a2_s.at[d], a2_r.at[t], (zz, f)).wait_send()

    pass_on(0)
    def share(d):
        tt = (t + d) % tcount
        if d:
            to(xbuf.at[c, tt], xbuf.at[c, tt], a2_r.at[tt], a2_r.at[tt], (t, sib)).wait_recv()
        send(xbuf.at[c, tt], xbuf.at[c, tt], a3_s.at[d], a3_r.at[tt], (t, sib))

    for d in range(1, fcount):
        got(bfb, (f + d) % fcount, bf_r)
    whole = bfb[0].astype(F32)
    for d in range(1, fcount):
        whole = whole + bfb[d].astype(F32)
    btb[t] = whole.astype(BF16)
    for d in range(1, tcount):
        send(btb.at[t], btb.at[t], bt_s.at[d], bt_r.at[t], ((t + d) % tcount, f))
    pass_on(1)
    pass_on(3)
    for d in range(1, tcount):
        got(btb, (t + d) % tcount, bt_r)
    band = btb[...].reshape(total, PANEL)
    eye = (
        lax.broadcasted_iota(jnp.int32, (PANEL, PANEL), 0) == lax.broadcasted_iota(jnp.int32, (PANEL, PANEL), 1)
    ).astype(F32)
    wa[0:PANEL, :] = dot0(band, band) / total + 0.1 * eye
    wi[0:PANEL, :] = eye
    wa[PANEL:, :] = jnp.zeros((PANEL, PANEL), F32)
    wi[PANEL:, :] = jnp.zeros((PANEL, PANEL), F32)

    def chol(lo, hi):
        @pl.loop(lo, hi)
        def _(ob):
            eliminate(ob, wa, wi)

    chol(0, 1)
    pass_on(2)
    for d in range(1, tcount):
        got(own, (t + d) % tcount, oc_r)
    wide = own[...].reshape(total, cols).astype(F32)
    wide = wide * wide
    fold = wide[:, 0:TILE]
    for v in range(1, cols // TILE):
        fold = fold + wide[:, v * TILE : (v + 1) * TILE]
    ssb[f] = lax.dot_general(
        jnp.ones((8, TILE), F32), fold, (((1,), (1,)), ((), ())), precision=HIGH, preferred_element_type=F32
    )
    for d in range(1, fcount):
        send(ssb.at[f], ssb.at[f], ss_s.at[d], ss_r.at[f], (t, (f + d) % fcount))
    chol(1, 3)
    share(0)
    share(1)
    share(3)
    share(2)

    width = 2 * cols

    def scaled(half):
        g = gain[:, pl.ds(pl.multiple_of(t * width + half * cols, cols), cols)]
        xg[half] = (xbuf[half].reshape(total, cols).astype(F32) * g).astype(BF16)

    load_gain.wait()
    scaled(c)
    for d in range(tcount):
        tt = (t + d) % tcount
        to(xbuf.at[1 - c, tt], xbuf.at[1 - c, tt], a3_r.at[tt], a3_r.at[tt], (t, sib)).wait_recv()
    scaled(1 - c)
    load.wait()
    for d in list(range(1, tcount)) + [0]:
        q = (t + d) % tcount
        at = pl.ds(pl.multiple_of(q * quarter, quarter), quarter)
        part = jnp.dot(xg[0], proj[0:cols, at], preferred_element_type=F32)
        part = part + jnp.dot(xg[1], proj[cols : 2 * cols, at], preferred_element_type=F32)
        if d:
            rss[q] = part.astype(BF16)
            send(rss.at[q], rsb.at[t], rs_s.at[d], rs_r.at[t], (q, f))
        else:
            accs[...] = part
    for d in range(1, fcount):
        got(ssb, (f + d) % fcount, ss_r)
    sums = ssb[0]
    for d in range(1, fcount):
        sums = sums + ssb[d]
    inv_row = lax.rsqrt(sums / (cols * fcount) + 1e-05)
    inv_ref[...] = dot0(inv_row, jnp.full((8, TILE), 0.125, F32), HIGH)
    chol(3, OUTER)
    linv = wi[0:PANEL, :]
    for d in range(1, tcount):
        got(rsb, (t + d) % tcount, rs_r)
    acc = accs[...]
    for d in range(1, tcount):
        acc = acc + rsb[(t + d) % tcount].astype(F32)
    inv2 = jnp.concatenate([inv_ref[...]] * (quarter // TILE), axis=1)
    mine = own[:, :, pl.ds(pl.multiple_of(t * quarter, quarter), quarter)].reshape(total, quarter).astype(F32)
    out = (mine + acc * inv2).astype(BF16)
    change = (out.astype(F32) - mine).astype(BF16)
    band = btb[...].reshape(total, PANEL)
    cross = dot0(band, change) * (math.sqrt(D) / total)
    result = jnp.dot(linv, cross, precision=HIGH, preferred_element_type=F32)
    agb[t] = result.astype(BF16)
    for d in range(1, tcount):
        send(agb.at[t], agb.at[t], ag_s.at[d], ag_r.at[t], ((t + d) % tcount, f))
    shape = (PANEL, quarter)
    for q in range(tcount):
        at = slice(q * quarter, (q + 1) * quarter)
        gram = dot0(band, own[:, :, at].reshape(total, quarter)) / total
        row_ids = lax.broadcasted_iota(jnp.int32, shape, 0)
        col_ids = lax.broadcasted_iota(jnp.int32, shape, 1) + (f * cols + q * quarter)
        gram = gram + jnp.where(col_ids == row_ids + start, 0.1, 0.0).astype(F32)
        panel[:, at] = jnp.dot(linv, gram, precision=HIGH, preferred_element_type=F32)
    solved[:, pl.ds(pl.multiple_of(t * quarter, quarter), quarter)] = result
    for d in range(1, tcount):
        q = (t + d) % tcount
        got(agb, q, ag_r)
        solved[:, pl.ds(pl.multiple_of(q * quarter, quarter), quarter)] = agb[q].astype(F32)
    for copy in sent:
        copy.wait_send()
    for d in range(zcount):
        pass_done(d)


def fused(tcount, fcount, tokens, gain, proj, panel_index):
    rows, cols = tokens.shape
    total, quarter, zcount = rows * tcount, cols // tcount, fcount // 2
    vmem = pl.BlockSpec(memory_space=pltpu.VMEM)
    dma = lambda n: pltpu.SemaphoreType.DMA((n,))
    scratch = [
        pltpu.VMEM(proj.shape, BF16),
        pltpu.VMEM((1, gain.shape[0]), F32),
        pltpu.VMEM((fcount, rows, PANEL), BF16),
        pltpu.VMEM((tcount, rows, PANEL), BF16),
        pltpu.VMEM((tcount, rows, cols), BF16),
        pltpu.VMEM((zcount, rows, cols), BF16),
        pltpu.VMEM((2, tcount, rows, cols), BF16),
        pltpu.VMEM((2, total, cols), BF16),
        pltpu.VMEM((fcount, 8, total), F32),
        pltpu.VMEM((tcount, total, quarter), BF16),
        pltpu.VMEM((tcount, total, quarter), BF16),
        pltpu.VMEM((tcount, PANEL, quarter), BF16),
        pltpu.VMEM((2 * PANEL, PANEL), F32),
        pltpu.VMEM((2 * PANEL, PANEL), F32),
        pltpu.VMEM((total, quarter), F32),
        pltpu.VMEM((total, TILE), F32),
        pltpu.SemaphoreType.DMA,
        pltpu.SemaphoreType.DMA,
        pltpu.SemaphoreType.DMA,
        pltpu.SemaphoreType.DMA,
    ]
    for n in (fcount, tcount, tcount, zcount, tcount, tcount, fcount, tcount, tcount):
        scratch += [dma(n), dma(n)]
    out = jax.ShapeDtypeStruct((PANEL, cols), F32)
    return pl.pallas_call(
        lambda *refs: kernel(tcount, fcount, *refs),
        out_shape=(out, out),
        in_specs=[pl.BlockSpec(memory_space=pl.ANY)] * 3 + [pl.BlockSpec(memory_space=pltpu.SMEM)],
        out_specs=(vmem, vmem),
        scratch_shapes=scratch,
        compiler_params=pltpu.CompilerParams(
            collective_id=0, has_side_effects=True, vmem_limit_bytes=62 * 1024 * 1024
        ),
    )(tokens, gain[None, :], proj, panel_index)

def solve_pair(factor, gram_part, cross_part):
    first = lax.linalg.triangular_solve(factor, gram_part, left_side=True, lower=True)
    second = lax.linalg.triangular_solve(factor, cross_part, left_side=True, lower=True)
    return (first, second)


def general(tokens, gain, proj, panel_index):
    token_full = lax.all_gather(tokens, "feat", axis=1, tiled=True)
    wide_rows = token_full.astype(jnp.float32)
    inv_rms = lax.rsqrt(jnp.mean(wide_rows * wide_rows, axis=1, keepdims=True) + 1e-05)
    normed = (wide_rows * inv_rms * gain[None, :]).astype(jnp.bfloat16)
    local_cols = tokens.shape[1]
    projected = jnp.dot(
        normed, lax.all_gather(proj, "tok", axis=0, tiled=True), preferred_element_type=jnp.float32
    )
    own_values = tokens.astype(jnp.float32)
    outputs = (own_values + projected).astype(jnp.bfloat16)
    change = (outputs.astype(jnp.float32) - own_values).astype(jnp.bfloat16)
    band_start = panel_index[0] * PANEL
    band_cols = lax.dynamic_slice_in_dim(token_full, band_start, PANEL, 1)
    gram_part = jnp.dot(band_cols.T, tokens, preferred_element_type=jnp.float32)
    cross_part = jnp.dot(band_cols.T, change, preferred_element_type=jnp.float32)
    gram_sum, cross_sum = (
        lax.psum_scatter(gram_part, "tok", scatter_dimension=0, tiled=True),
        lax.psum_scatter(cross_part, "tok", scatter_dimension=0, tiled=True),
    )
    tok_count = lax.axis_size("tok")
    feat_count = lax.axis_size("feat")
    token_count = tokens.shape[0] * tok_count
    rows_here = gram_sum.shape[0]
    row_ids = lax.broadcasted_iota(jnp.int32, gram_sum.shape, 0) + lax.axis_index("tok") * rows_here
    col_ids = (
        lax.broadcasted_iota(jnp.int32, gram_sum.shape, 1) + lax.axis_index("feat") * local_cols
    )
    ridge_mask = jnp.where(col_ids == row_ids + band_start, 0.1, 0.0).astype(jnp.float32)
    gram_rows = gram_sum / token_count + ridge_mask
    cross_rows = cross_sum * (math.sqrt(D) / token_count)
    slab_rows = PANEL // feat_count
    own_slab = lax.dynamic_slice_in_dim(band_cols, lax.axis_index("feat") * slab_rows, slab_rows, 1)
    partial_value = jnp.dot(own_slab.T, band_cols, preferred_element_type=jnp.float32)
    summed = lax.psum(partial_value, "tok")
    diag_sum = lax.all_gather(summed, "feat", axis=0, tiled=True)
    diag_block = diag_sum / token_count + 0.1 * jnp.eye(PANEL, dtype=jnp.float32)
    factor = jnp.linalg.cholesky(diag_block)
    gram_some, cross_some = (
        lax.all_to_all(gram_rows, "tok", split_axis=1, concat_axis=0, tiled=True),
        lax.all_to_all(cross_rows, "tok", split_axis=1, concat_axis=0, tiled=True),
    )
    panel_some, solved_some = solve_pair(factor, gram_some, cross_some)
    panel_rows, solved_cross = (
        lax.all_gather(panel_some, "tok", axis=1, tiled=True),
        lax.all_gather(solved_some, "tok", axis=1, tiled=True),
    )
    return (panel_rows, solved_cross)


def solution(mesh):
    tcount, fcount = mesh.shape["tok"], mesh.shape["feat"]

    def body(tokens, gain, proj, panel_index):
        rows, cols = tokens.shape
        fits = (
            fcount == 2 * tcount
            and proj.shape[0] == 2 * cols
            and rows % 16 == 0
            and rows * tcount == PANEL
            and cols % (tcount * TILE) == 0
            and cols % PANEL == 0
        )
        if fits:
            return fused(tcount, fcount, tokens, gain, proj, panel_index)
        return general(tokens, gain, proj, panel_index)

    return jax.shard_map(
        body,
        mesh=mesh,
        in_specs=(P("tok", "feat"), P(), P("tok", "feat"), P()),
        out_specs=(P(None, "feat"), P(None, "feat")),
        check_vma=False,
    )
```

```python
import math

import jax
import jax.numpy as jnp
from jax import lax
from jax.experimental import pallas as pl
from jax.experimental.pallas import tpu as pltpu
from jax.sharding import PartitionSpec as P

D = 8192
PANEL = 256
MESH = pl.DeviceIdType.MESH
HIGH = lax.Precision.HIGHEST
F32 = jnp.float32
BF16 = jnp.bfloat16
STEP = 32
TILE = 128
OUTER = PANEL // STEP
REST = PANEL - STEP


def dot0(a, b, precision=None):
    return lax.dot_general(a, b, (((0,), (0,)), ((), ())), precision=precision, preferred_element_type=F32)


def lanes(col):
    return jnp.broadcast_to(col, (8, TILE))


def eliminate(ob, wa, wi):
    r0 = pl.multiple_of(ob * STEP, STEP)
    groups = []
    for g in range(STEP // 8):
        rows = pl.ds(pl.multiple_of(r0 + 8 * g, 8), 8)
        groups.append(
            [wa[rows, 0:128], wa[rows, 128:256], wi[rows, 0:128], wi[rows, 128:256]]
        )
    sub = lax.broadcasted_iota(jnp.int32, (8, TILE), 0)
    n = STEP // 8
    for k in range(n):
        cols = {
            g: [lanes(groups[g][0][:, 8 * k + j : 8 * k + j + 1]) for j in range(8)]
            for g in range(k, n)
        }
        a = [[lanes(cols[k][j][i : i + 1, :]) if j <= i else None for j in range(8)] for i in range(8)]
        low = [[None] * 8 for _ in range(8)]
        inv = [None] * 8
        for j in range(8):
            inv[j] = lax.rsqrt(a[j][j])
            for i in range(j + 1, 8):
                low[i][j] = a[i][j] * inv[j]
            for l in range(j + 1, 8):
                for i in range(l, 8):
                    a[i][l] = a[i][l] - low[i][j] * low[l][j]
        m = [[None] * 8 for _ in range(8)]
        for j in range(8):
            m[j][j] = inv[j]
            for i in range(j + 1, 8):
                acc = low[i][j] * m[j][j]
                for l in range(j + 1, i):
                    acc = acc + low[i][l] * m[l][j]
                m[i][j] = -inv[i] * acc
        zero = jnp.zeros((8, TILE), F32)
        mcol, mrow = [], []
        for j in range(8):
            c = zero
            for i in range(j, 8):
                c = jnp.where(sub == i, m[i][j], c)
            mcol.append(c)
        for i in range(8):
            c = zero
            for j in range(0, i + 1):
                c = jnp.where(sub == j, m[i][j], c)
            mrow.append(c)
        done = []
        for v in range(4):
            r = groups[k][v]
            u = mcol[0] * lanes(r[0:1, :])
            for j in range(1, 8):
                u = u + mcol[j] * lanes(r[j : j + 1, :])
            done.append(u)
            if k < n - 1:
                w = mrow[0] * lanes(u[0:1, :])
                for j in range(1, 8):
                    w = w + mrow[j] * lanes(u[j : j + 1, :])
                wb = [lanes(w[j : j + 1, :]) for j in range(8)]
                for g in range(k + 1, n):
                    s = cols[g][0] * wb[0]
                    for j in range(1, 8):
                        s = s + cols[g][j] * wb[j]
                    groups[g][v] = groups[g][v] - s
        groups[k] = done
    for g in range(n):
        rows = pl.ds(pl.multiple_of(r0 + 8 * g, 8), 8)
        wi[rows, 0:128] = groups[g][2]
        wi[rows, 128:256] = groups[g][3]
    ua = jnp.concatenate(
        [jnp.concatenate([groups[g][0] for g in range(n)], axis=0), jnp.concatenate([groups[g][1] for g in range(n)], axis=0)],
        axis=1,
    )
    ui = jnp.concatenate(
        [jnp.concatenate([groups[g][2] for g in range(n)], axis=0), jnp.concatenate([groups[g][3] for g in range(n)], axis=0)],
        axis=1,
    )
    rest = pl.ds(pl.multiple_of(r0 + STEP, STEP), REST)
    left = ua[:, STEP:]
    if STEP % 128:
        left = pltpu.roll(ua, PANEL - STEP, 1)
    wa[rest, :] = pltpu.roll(wa[rest, :] - dot0(left, ua, HIGH)[:REST], PANEL - STEP, 1)
    wi[rest, :] = wi[rest, :] - dot0(left, ui, HIGH)[:REST]


def kernel(
    tcount, fcount, tokens, gain_hbm, proj_hbm, pidx, panel, solved,
    proj, gain, bfb, btb, own, zbuf, xbuf, xg, ssb, rsb, rss, agb, wa, wi, accs, inv_ref,
    proj_sem, gain_sem, own_sem, z_sem, bf_s, bf_r, bt_s, bt_r, oc_s, oc_r, a1_s, a1_r, a2_s, a2_r, a3_s, a3_r,
    ss_s, ss_r, rs_s, rs_r, ag_s, ag_r,
):
    t = lax.axis_index("tok")
    f = lax.axis_index("feat")
    z, c = f // 2, f % 2
    sib = f + 1 - 2 * c
    zcount = fcount // 2
    rows, cols = tokens.shape
    total = rows * tcount
    quarter = cols // tcount

    load = pltpu.make_async_copy(proj_hbm, proj, proj_sem)
    start = pidx[0] * PANEL
    load_own = pltpu.make_async_copy(tokens, own.at[t], own_sem)
    load_own.start()
    load_z = pltpu.make_async_copy(tokens, zbuf.at[z], z_sem)
    load_z.start()
    load_gain = pltpu.make_async_copy(gain_hbm, gain, gain_sem)
    load_gain.start()
    load.start()
    barrier = pltpu.get_barrier_semaphore()
    for d in range(1, fcount):
        pl.semaphore_signal(barrier, inc=1, device_id=(t, (f + d) % fcount), device_id_type=MESH)
    for d in range(1, tcount):
        pl.semaphore_signal(barrier, inc=1, device_id=((t + d) % tcount, f), device_id_type=MESH)
    shape = (cols, PANEL)
    pick = lax.broadcasted_iota(jnp.int32, shape, 0) + f * cols == lax.broadcasted_iota(jnp.int32, shape, 1) + start
    pick = jnp.where(pick, 1.0, 0.0).astype(BF16)
    load_own.wait()
    bfb[f] = jnp.dot(own[t], pick, preferred_element_type=F32).astype(BF16)
    load_z.wait()
    pl.semaphore_wait(barrier, fcount + tcount - 2)

    def to(src, dst, ssem, rsem, device):
        return pltpu.make_async_remote_copy(
            src_ref=src, dst_ref=dst, send_sem=ssem, recv_sem=rsem, device_id=device, device_id_type=MESH
        )

    sent = []

    def send(src, dst, ssem, rsem, device):
        copy = to(src, dst, ssem, rsem, device)
        copy.start()
        sent.append(copy)

    def got(buf, slot, rsem):
        to(buf.at[slot], buf.at[slot], rsem.at[slot], rsem.at[slot], (t, sib)).wait_recv()

    for d in range(1, fcount):
        send(bfb.at[f], bfb.at[f], bf_s.at[d], bf_r.at[f], (t, (f + d) % fcount))
    for d in range(1, tcount):
        send(own.at[t], own.at[t], oc_s.at[d], oc_r.at[t], ((t + d) % tcount, f))
    for d in range(1, zcount):
        send(zbuf.at[z], zbuf.at[z], a1_s.at[d], a1_r.at[z], (t, ((z + d) % zcount) * 2 + c))

    def pass_on(d):
        zz = (z + d) % zcount
        if d:
            got(zbuf, zz, a1_r)

        @pl.when(zz == t)
        def _():
            xbuf[c, t] = zbuf[zz]

        @pl.when(zz != t)
        def _():
            to(zbuf.at[zz], xbuf.at[c, t], a2_s.at[d], a2_r.at[t], (zz, f)).start()

    def pass_done(d):
        zz = (z + d) % zcount

        @pl.when(zz != t)
        def _():
            to(zbuf.at[zz], xbuf.at[c, t], a2_s.at[d], a2_r.at[t], (zz, f)).wait_send()

    pass_on(0)
    def share(d):
        tt = (t + d) % tcount
        if d:
            to(xbuf.at[c, tt], xbuf.at[c, tt], a2_r.at[tt], a2_r.at[tt], (t, sib)).wait_recv()
        send(xbuf.at[c, tt], xbuf.at[c, tt], a3_s.at[d], a3_r.at[tt], (t, sib))

    for d in range(1, fcount):
        got(bfb, (f + d) % fcount, bf_r)
    whole = bfb[0].astype(F32)
    for d in range(1, fcount):
        whole = whole + bfb[d].astype(F32)
    btb[t] = whole.astype(BF16)
    for d in range(1, tcount):
        send(btb.at[t], btb.at[t], bt_s.at[d], bt_r.at[t], ((t + d) % tcount, f))
    pass_on(1)
    pass_on(3)
    for d in range(1, tcount):
        got(btb, (t + d) % tcount, bt_r)
    band = btb[...].reshape(total, PANEL)
    eye = (
        lax.broadcasted_iota(jnp.int32, (PANEL, PANEL), 0) == lax.broadcasted_iota(jnp.int32, (PANEL, PANEL), 1)
    ).astype(F32)
    wa[0:PANEL, :] = dot0(band, band) / total + 0.1 * eye
    wi[0:PANEL, :] = eye
    wa[PANEL:, :] = jnp.zeros((PANEL, PANEL), F32)
    wi[PANEL:, :] = jnp.zeros((PANEL, PANEL), F32)

    def chol(lo, hi):
        @pl.loop(lo, hi)
        def _(ob):
            eliminate(ob, wa, wi)

    chol(0, 1)
    pass_on(2)
    for d in range(1, tcount):
        got(own, (t + d) % tcount, oc_r)
    wide = own[...].reshape(total, cols).astype(F32)
    wide = wide * wide
    fold = wide[:, 0:TILE]
    for v in range(1, cols // TILE):
        fold = fold + wide[:, v * TILE : (v + 1) * TILE]
    ssb[f] = lax.dot_general(
        jnp.ones((8, TILE), F32), fold, (((1,), (1,)), ((), ())), precision=HIGH, preferred_element_type=F32
    )
    for d in range(1, fcount):
        send(ssb.at[f], ssb.at[f], ss_s.at[d], ss_r.at[f], (t, (f + d) % fcount))
    chol(1, 4)
    share(0)
    share(1)
    share(3)
    share(2)

    width = 2 * cols

    def scaled(half):
        g = gain[:, pl.ds(pl.multiple_of(t * width + half * cols, cols), cols)]
        xg[half] = (xbuf[half].reshape(total, cols).astype(F32) * g).astype(BF16)

    load_gain.wait()
    scaled(c)
    for d in range(tcount):
        tt = (t + d) % tcount
        to(xbuf.at[1 - c, tt], xbuf.at[1 - c, tt], a3_r.at[tt], a3_r.at[tt], (t, sib)).wait_recv()
    scaled(1 - c)
    load.wait()
    for d in list(range(1, tcount)) + [0]:
        q = (t + d) % tcount
        at = pl.ds(pl.multiple_of(q * quarter, quarter), quarter)
        part = jnp.dot(xg[0], proj[0:cols, at], preferred_element_type=F32)
        part = part + jnp.dot(xg[1], proj[cols : 2 * cols, at], preferred_element_type=F32)
        if d:
            rss[q] = part.astype(BF16)
            send(rss.at[q], rsb.at[t], rs_s.at[d], rs_r.at[t], (q, f))
        else:
            accs[...] = part
    for d in range(1, fcount):
        got(ssb, (f + d) % fcount, ss_r)
    sums = ssb[0]
    for d in range(1, fcount):
        sums = sums + ssb[d]
    inv_row = lax.rsqrt(sums / (cols * fcount) + 1e-05)
    inv_ref[...] = dot0(inv_row, jnp.full((8, TILE), 0.125, F32), HIGH)
    chol(4, OUTER)
    linv = wi[0:PANEL, :]
    for d in range(1, tcount):
        got(rsb, (t + d) % tcount, rs_r)
    acc = accs[...]
    for d in range(1, tcount):
        acc = acc + rsb[(t + d) % tcount].astype(F32)
    inv2 = jnp.concatenate([inv_ref[...]] * (quarter // TILE), axis=1)
    mine = own[:, :, pl.ds(pl.multiple_of(t * quarter, quarter), quarter)].reshape(total, quarter).astype(F32)
    out = (mine + acc * inv2).astype(BF16)
    change = (out.astype(F32) - mine).astype(BF16)
    band = btb[...].reshape(total, PANEL)
    cross = dot0(band, change) * (math.sqrt(D) / total)
    result = jnp.dot(linv, cross, precision=HIGH, preferred_element_type=F32)
    agb[t] = result.astype(BF16)
    for d in range(1, tcount):
        send(agb.at[t], agb.at[t], ag_s.at[d], ag_r.at[t], ((t + d) % tcount, f))
    shape = (PANEL, quarter)
    for q in range(tcount):
        at = slice(q * quarter, (q + 1) * quarter)
        gram = dot0(band, own[:, :, at].reshape(total, quarter)) / total
        row_ids = lax.broadcasted_iota(jnp.int32, shape, 0)
        col_ids = lax.broadcasted_iota(jnp.int32, shape, 1) + (f * cols + q * quarter)
        gram = gram + jnp.where(col_ids == row_ids + start, 0.1, 0.0).astype(F32)
        panel[:, at] = jnp.dot(linv, gram, precision=HIGH, preferred_element_type=F32)
    solved[:, pl.ds(pl.multiple_of(t * quarter, quarter), quarter)] = result
    for d in range(1, tcount):
        q = (t + d) % tcount
        got(agb, q, ag_r)
        solved[:, pl.ds(pl.multiple_of(q * quarter, quarter), quarter)] = agb[q].astype(F32)
    for copy in sent:
        copy.wait_send()
    for d in range(zcount):
        pass_done(d)


def fused(tcount, fcount, tokens, gain, proj, panel_index):
    rows, cols = tokens.shape
    total, quarter, zcount = rows * tcount, cols // tcount, fcount // 2
    vmem = pl.BlockSpec(memory_space=pltpu.VMEM)
    dma = lambda n: pltpu.SemaphoreType.DMA((n,))
    scratch = [
        pltpu.VMEM(proj.shape, BF16),
        pltpu.VMEM((1, gain.shape[0]), F32),
        pltpu.VMEM((fcount, rows, PANEL), BF16),
        pltpu.VMEM((tcount, rows, PANEL), BF16),
        pltpu.VMEM((tcount, rows, cols), BF16),
        pltpu.VMEM((zcount, rows, cols), BF16),
        pltpu.VMEM((2, tcount, rows, cols), BF16),
        pltpu.VMEM((2, total, cols), BF16),
        pltpu.VMEM((fcount, 8, total), F32),
        pltpu.VMEM((tcount, total, quarter), BF16),
        pltpu.VMEM((tcount, total, quarter), BF16),
        pltpu.VMEM((tcount, PANEL, quarter), BF16),
        pltpu.VMEM((2 * PANEL, PANEL), F32),
        pltpu.VMEM((2 * PANEL, PANEL), F32),
        pltpu.VMEM((total, quarter), F32),
        pltpu.VMEM((total, TILE), F32),
        pltpu.SemaphoreType.DMA,
        pltpu.SemaphoreType.DMA,
        pltpu.SemaphoreType.DMA,
        pltpu.SemaphoreType.DMA,
    ]
    for n in (fcount, tcount, tcount, zcount, tcount, tcount, fcount, tcount, tcount):
        scratch += [dma(n), dma(n)]
    out = jax.ShapeDtypeStruct((PANEL, cols), F32)
    return pl.pallas_call(
        lambda *refs: kernel(tcount, fcount, *refs),
        out_shape=(out, out),
        in_specs=[pl.BlockSpec(memory_space=pl.ANY)] * 3 + [pl.BlockSpec(memory_space=pltpu.SMEM)],
        out_specs=(vmem, vmem),
        scratch_shapes=scratch,
        compiler_params=pltpu.CompilerParams(
            collective_id=0, has_side_effects=True, vmem_limit_bytes=48 * 1024 * 1024
        ),
    )(tokens, gain[None, :], proj, panel_index)

def solve_pair(factor, gram_part, cross_part):
    first = lax.linalg.triangular_solve(factor, gram_part, left_side=True, lower=True)
    second = lax.linalg.triangular_solve(factor, cross_part, left_side=True, lower=True)
    return (first, second)


def general(tokens, gain, proj, panel_index):
    token_full = lax.all_gather(tokens, "feat", axis=1, tiled=True)
    wide_rows = token_full.astype(jnp.float32)
    inv_rms = lax.rsqrt(jnp.mean(wide_rows * wide_rows, axis=1, keepdims=True) + 1e-05)
    normed = (wide_rows * inv_rms * gain[None, :]).astype(jnp.bfloat16)
    local_cols = tokens.shape[1]
    projected = jnp.dot(
        normed, lax.all_gather(proj, "tok", axis=0, tiled=True), preferred_element_type=jnp.float32
    )
    own_values = tokens.astype(jnp.float32)
    outputs = (own_values + projected).astype(jnp.bfloat16)
    change = (outputs.astype(jnp.float32) - own_values).astype(jnp.bfloat16)
    band_start = panel_index[0] * PANEL
    band_cols = lax.dynamic_slice_in_dim(token_full, band_start, PANEL, 1)
    gram_part = jnp.dot(band_cols.T, tokens, preferred_element_type=jnp.float32)
    cross_part = jnp.dot(band_cols.T, change, preferred_element_type=jnp.float32)
    gram_sum, cross_sum = (
        lax.psum_scatter(gram_part, "tok", scatter_dimension=0, tiled=True),
        lax.psum_scatter(cross_part, "tok", scatter_dimension=0, tiled=True),
    )
    tok_count = lax.axis_size("tok")
    feat_count = lax.axis_size("feat")
    token_count = tokens.shape[0] * tok_count
    rows_here = gram_sum.shape[0]
    row_ids = lax.broadcasted_iota(jnp.int32, gram_sum.shape, 0) + lax.axis_index("tok") * rows_here
    col_ids = (
        lax.broadcasted_iota(jnp.int32, gram_sum.shape, 1) + lax.axis_index("feat") * local_cols
    )
    ridge_mask = jnp.where(col_ids == row_ids + band_start, 0.1, 0.0).astype(jnp.float32)
    gram_rows = gram_sum / token_count + ridge_mask
    cross_rows = cross_sum * (math.sqrt(D) / token_count)
    slab_rows = PANEL // feat_count
    own_slab = lax.dynamic_slice_in_dim(band_cols, lax.axis_index("feat") * slab_rows, slab_rows, 1)
    partial_value = jnp.dot(own_slab.T, band_cols, preferred_element_type=jnp.float32)
    summed = lax.psum(partial_value, "tok")
    diag_sum = lax.all_gather(summed, "feat", axis=0, tiled=True)
    diag_block = diag_sum / token_count + 0.1 * jnp.eye(PANEL, dtype=jnp.float32)
    factor = jnp.linalg.cholesky(diag_block)
    gram_some, cross_some = (
        lax.all_to_all(gram_rows, "tok", split_axis=1, concat_axis=0, tiled=True),
        lax.all_to_all(cross_rows, "tok", split_axis=1, concat_axis=0, tiled=True),
    )
    panel_some, solved_some = solve_pair(factor, gram_some, cross_some)
    panel_rows, solved_cross = (
        lax.all_gather(panel_some, "tok", axis=1, tiled=True),
        lax.all_gather(solved_some, "tok", axis=1, tiled=True),
    )
    return (panel_rows, solved_cross)


def solution(mesh):
    tcount, fcount = mesh.shape["tok"], mesh.shape["feat"]

    def body(tokens, gain, proj, panel_index):
        rows, cols = tokens.shape
        fits = (
            fcount == 2 * tcount
            and proj.shape[0] == 2 * cols
            and rows % 16 == 0
            and rows * tcount == PANEL
            and cols % (tcount * TILE) == 0
            and cols % PANEL == 0
        )
        if fits:
            return fused(tcount, fcount, tokens, gain, proj, panel_index)
        return general(tokens, gain, proj, panel_index)

    return jax.shard_map(
        body,
        mesh=mesh,
        in_specs=(P("tok", "feat"), P(), P("tok", "feat"), P()),
        out_specs=(P(None, "feat"), P(None, "feat")),
        check_vma=False,
    )
```
